32 devices in a mesh: groups: 2 (over y), loop: 4 (over z), enc: 2 (over x), rep: 2 (over core).
Axes of the slice: x: 2, y: 2, z: 4, core: 2. Of those that a mesh axis runs over, the one named last changes fastest.
Arguments:
- embeddings: bfloat16 [4096, 768], P(('groups', 'loop', 'rep'), 'enc'), parts along dimension 0, may hold values from -24 to 24
- head_weight: bfloat16 [768, 768], P('enc'), may hold values from -0.21875 to 0.21875
- gp_weights: float32 [4096], P('groups'), parts along dimension 0, may hold values from -24 to 24
- counts: int32 [8], P('groups'), parts along dimension 0, may hold values from 64 to 512, as said below
Outputs:
- embed_grad: bfloat16 [4096, 768], P(('groups', 'loop', 'rep'), 'enc'), parts along dimension 0
- head_grad: float32 [1536, 768], P(('groups', 'enc')), parts along dimension 0
The draws below stay inside these ranges and needn't reach their ends.
There are 2 independent parts, one for each index of `groups`. The reference program is written for one: setup_inputs(seed, part) draws one part's arguments, and reference() takes and returns one part's arrays. A program takes and returns all parts, laid end to end along the dimension named above; an argument that names none is the same for every part. Nothing has to cross between parts.
Inputs may be any that keep to these rules, and one draw needn't show every extreme that they name: `counts`: some block is full and some block holds exactly 64 valid molecules.
All inputs are finite; a program needn't handle non-finite values.
Results may differ from the reference program's by a relative error of at most 0.019.
Values may be sent and summed in bfloat16 or wider, within the bound.
A program may use at most 64 MiB of HBM per device.

```python
import math
import jax
import jax.numpy as jnp
from jax import lax

E = 768
F = 768
BLOCK = 512
BLOCKS = 4
MOLS = 2048


def draw_embeddings(key, part):
    key = jax.random.fold_in(key, 11)
    key_base = jax.random.fold_in(key, 0)
    key_rows = jax.random.fold_in(key, 1)
    key_cols = jax.random.fold_in(key, 3)
    row_scale = jnp.exp(jax.random.uniform(key_rows, (MOLS, 1), jnp.float32, math.log(0.3), math.log(3.0)))
    col_scale = jnp.exp(jax.random.uniform(key_cols, (1, E), jnp.float32, math.log(0.5), math.log(2.0)))
    base = jax.random.normal(key_base, (MOLS, E), jnp.float32)
    base = jnp.clip(base, -4.0, 4.0)
    return (base * row_scale * col_scale).astype(jnp.bfloat16)


def draw_counts(key, part):
    key = jax.random.fold_in(key, 7)
    key_draw, key_full, key_low = jax.random.split(key, 3)
    values = jax.random.randint(key_draw, (BLOCKS,), BLOCK // 8, BLOCK + 1)
    full_at = jax.random.randint(key_full, (), 0, BLOCKS)
    low_at = (full_at + 1 + jax.random.randint(key_low, (), 0, BLOCKS - 1)) % BLOCKS
    values = values.at[full_at].set(BLOCK).at[low_at].set(BLOCK // 8)
    return values.astype(jnp.int32)


def level_of(stream_key, dims, pieces, low, top_value):
    factor_of = 1.0
    for dim, shards_of in pieces:
        steps = jax.random.uniform(jax.random.fold_in(jax.random.fold_in(stream_key, 6), dim), (shards_of,), jnp.float32, low / len(pieces), top_value / len(pieces))
        factor_of = factor_of * jnp.repeat(jnp.exp(steps), dims[dim] // shards_of).reshape((-1,) + (1,) * (len(dims) - 1 - dim))
    return factor_of


def centred(key, shape, width, reach, pieces=(), kind=jnp.bfloat16):
    loudness = level_of(key, shape, pieces, -0.22, 0.18) if pieces else 1.0
    drawn = jax.random.normal(key, shape, jnp.float32) * width * loudness
    return jnp.minimum(jnp.maximum(drawn, -reach), reach).astype(kind)


def setup_inputs(seed: int = 0, part: int = 0) -> dict:
    streams_of = jax.random.split(jax.random.key(seed), 5)
    part_keys = jax.random.split(jax.random.fold_in(streams_of[4], part), 5)
    embeddings = draw_embeddings(jax.random.fold_in(jax.random.fold_in(streams_of[4], part), 71), part)
    head_weight = centred(streams_of[1], (E, F), E ** -0.5, 0.21875, ((0, 2),))
    gp_weights = centred(part_keys[2], (MOLS,), 4.0, 24.0, (), jnp.float32)
    counts = draw_counts(jax.random.fold_in(jax.random.fold_in(streams_of[4], part), 71), part)
    return {"embeddings": embeddings, "head_weight": head_weight, "gp_weights": gp_weights, "counts": counts}


EPSILON = 1e-6


def reference(embeddings, head_weight, gp_weights, counts):
    features = jnp.dot(embeddings, head_weight, preferred_element_type=jnp.float32).astype(jnp.bfloat16)
    wide = features.astype(jnp.float32)
    norms = jnp.sum(wide * wide, axis=1)
    total = embeddings.shape[0]
    rows_all = jnp.arange(total, dtype=jnp.int32)
    block_of = rows_all // BLOCK
    inside = rows_all % BLOCK
    limit = counts[block_of]
    weights = jnp.where(inside < limit, gp_weights, jnp.zeros_like(gp_weights))

    def one_block(block_index):
        start = (block_index * BLOCK).astype(jnp.int32)
        left = lax.dynamic_slice_in_dim(features, start, BLOCK, 0)
        left_norms = lax.dynamic_slice_in_dim(norms, start, BLOCK, 0)
        left_weights = lax.dynamic_slice_in_dim(weights, start, BLOCK, 0)
        scores = jnp.dot(left, features.T, preferred_element_type=jnp.float32)
        denom = left_norms[:, None] + norms[None, :] - scores + EPSILON
        inverse = 1.0 / (denom * denom)
        pair_coef = left_weights[:, None] * weights[None, :]
        pair_weight = (pair_coef * (left_norms[:, None] + norms[None, :]) * inverse).astype(jnp.bfloat16)
        quotient = jnp.sum(pair_coef * 2.0 * scores * inverse, axis=1)
        carried = jnp.dot(pair_weight, features, preferred_element_type=jnp.float32)
        return carried - left.astype(jnp.float32) * quotient[:, None]

    grads = lax.map(one_block, jnp.arange(total // BLOCK, dtype=jnp.int32))
    grad_features = grads.reshape(total, features.shape[1])
    feature_grad = grad_features.astype(jnp.bfloat16)
    embed_grad = jnp.dot(feature_grad, head_weight.T, preferred_element_type=jnp.float32).astype(jnp.bfloat16)
    head_grad = jnp.dot(embeddings.T, feature_grad, preferred_element_type=jnp.float32)
    return embed_grad, head_grad
```

```python
import functools

import jax
import jax.numpy as jnp
from jax import lax
from jax.experimental import pallas as pl
from jax.experimental.pallas import tpu as pltpu
from jax.sharding import PartitionSpec as P

EPSILON = 1e-06
PARTS = 3
MESH_ID = pl.DeviceIdType.MESH


def kernel(
    sizes,
    emb_ref,
    head_ref,
    gp_ref,
    counts_ref,
    embed_out,
    head_out,
    e_all,
    w_all,
    f_own,
    n_own,
    accum,
    quot,
    h_own,
    h_core,
    h_recv,
    h_send,
    h_side,
    h_full,
    e_recv,
    z_send,
    zx_send,
    x_send,
    c_send,
    w_send,
    w_recv,
    wc_send,
    wc_recv,
    hc_send,
    hc_recv,
    hi_send,
    hi_recv,
    ho_send,
    hf_send,
    hf_recv,
):
    nz, nx, nc = sizes
    z = lax.axis_index("loop")
    x = lax.axis_index("enc")
    c = lax.axis_index("rep")
    other = 1 - c
    pair = z + 1 - 2 * lax.rem(z, 2)
    rows = emb_ref.shape[0]
    half, feats = w_all.shape[2], w_all.shape[3]
    width = feats // PARTS
    has_left = z > 0
    has_right = z < nz - 1

    def x_peer(j):
        return lax.rem(x + 1 + j, nx)

    def remote(src, dst, send, recv, device):
        return pltpu.make_async_remote_copy(
            src_ref=src, dst_ref=dst, send_sem=send, recv_sem=recv,
            device_id=device, device_id_type=MESH_ID,
        )

    def e_copy(b, cc, xx, send, device):
        slot = e_all.at[b, cc, xx]
        return remote(slot, slot, send, e_recv.at[b, cc, xx], device)

    def z_copy(b, d):
        return e_copy(b, c, x, z_send.at[d, b], {"loop": z + (1 if d == 0 else -1)})

    def zx_copy(j):
        return e_copy(z, c, x_peer(j), zx_send.at[j], {"loop": pair})

    def x_copy(b, j):
        return e_copy(b, c, x, x_send.at[j, b], {"enc": x_peer(j)})

    def c_copy(b, xx):
        return e_copy(b, c, xx, c_send.at[b, xx], {"rep": other})

    def e_wait(b, cc, xx):
        e_copy(b, cc, xx, c_send.at[b, xx], {"rep": other}).wait_recv()

    def w_copy(j):
        slot = w_all.at[x, c]
        return remote(slot, slot, w_send.at[j], w_recv.at[x], {"enc": x_peer(j)})

    def wc_copy(j):
        slot = w_all.at[x_peer(j), c]
        return remote(slot, slot, wc_send.at[j], wc_recv.at[j], {"rep": other})

    barrier = pltpu.get_barrier_semaphore()

    @pl.when(has_left)
    def _():
        pl.semaphore_signal(barrier, 1, device_id={"loop": z - 1}, device_id_type=MESH_ID)

    @pl.when(has_right)
    def _():
        pl.semaphore_signal(barrier, 1, device_id={"loop": z + 1}, device_id_type=MESH_ID)

    for j in range(nx - 1):
        pl.semaphore_signal(barrier, 1, device_id={"enc": x_peer(j)}, device_id_type=MESH_ID)
    pl.semaphore_signal(barrier, 1, device_id={"rep": other}, device_id_type=MESH_ID)

    e_all[z, c, x] = emb_ref[...]
    for cc in range(nc):
        w_all[x, cc] = head_ref[cc * half : (cc + 1) * half, :]
    accum[...] = jnp.zeros_like(accum)
    quot[...] = jnp.zeros_like(quot)

    pl.semaphore_wait(
        barrier, nx + has_left.astype(jnp.int32) + has_right.astype(jnp.int32)
    )

    def features(b, cc):
        total = jnp.dot(
            e_all[b, cc, 0], w_all[0].reshape(nc * half, feats),
            preferred_element_type=jnp.float32,
        )
        for xx in range(1, nx):
            total = total + jnp.dot(
                e_all[b, cc, xx], w_all[xx].reshape(nc * half, feats),
                preferred_element_type=jnp.float32,
            )
        total = total.astype(jnp.bfloat16)
        wide = total.astype(jnp.float32)
        return total, jnp.sum(wide * wide, axis=1, keepdims=True)

    def eye():
        return lax.broadcasted_iota(jnp.int32, (rows, rows), 0) == lax.broadcasted_iota(
            jnp.int32, (rows, rows), 1
        )

    def weight_row(b, cc):
        place = cc * rows + lax.broadcasted_iota(jnp.int32, (1, rows), 1)
        return jnp.where(place < counts_ref[b], gp_ref[pl.ds(b * nc + cc, 1), :], 0.0)

    def tile(b, cc, feat, norm):
        norm_row = jnp.sum(jnp.where(eye(), norm, 0.0), axis=0, keepdims=True)
        scores = lax.dot_general(
            f_own[...], feat, (((1,), (1,)), ((), ())), preferred_element_type=jnp.float32
        )
        both = n_own[...] + norm_row
        denom = both - scores + EPSILON
        scaled = weight_row(b, cc) * (1.0 / (denom * denom))
        quot[...] += jnp.sum(scaled * scores, axis=1, keepdims=True)
        accum[...] += jnp.dot(
            (both * scaled).astype(jnp.bfloat16), feat, preferred_element_type=jnp.float32
        )

    def stage_z(s, d):
        b = z - s if d == 0 else z + s
        valid = jnp.logical_and(b >= 0, b < nz)
        if d == 1:
            valid = jnp.logical_and(valid, s > 0)

        @pl.when(valid)
        def _():
            @pl.when(s > 0)
            def _():
                e_wait(b, c, x)

            @pl.when(jnp.logical_or(s == 0, has_right if d == 0 else has_left))
            def _():
                if d == 0:
                    @pl.when(has_right)
                    def _():
                        z_copy(b, 0).start()

                    @pl.when(jnp.logical_and(s == 0, has_left))
                    def _():
                        z_copy(b, 1).start()
                else:
                    z_copy(b, 1).start()

            @pl.when(b != pair)
            def _():
                for j in range(nx - 1):
                    x_copy(b, j).start()

            c_copy(b, x).start()

            @pl.when(s == 0)
            def _():
                for j in range(nx - 1):
                    w_copy(j).start()

    def stage_x(s, d):
        b = z - s if d == 0 else z + s
        valid = jnp.logical_and(jnp.logical_and(b >= 0, b < nz), s >= (1 if d else 0))

        @pl.when(valid)
        def _():
            for j in range(nx - 1):
                e_wait(b, c, x_peer(j))

                @pl.when(s == 0)
                def _():
                    zx_copy(j).start()

                c_copy(b, x_peer(j)).start()

    def stage_c(s, d):
        b = z - s if d == 0 else z + s
        valid = jnp.logical_and(jnp.logical_and(b >= 0, b < nz), s >= (1 if d else 0))

        @pl.when(valid)
        def _():
            @pl.when(s == 0)
            def _():
                for j in range(nx - 1):
                    peer = x_peer(j)
                    slot = w_all.at[peer, c]
                    remote(
                        slot, slot, w_send.at[j], w_recv.at[peer], {"enc": peer}
                    ).wait_recv()
                    wc_copy(j).start()
                for j in range(nx - 1):
                    slot = w_all.at[x_peer(j), other]
                    remote(
                        slot, slot, wc_send.at[j], wc_recv.at[j], {"rep": other}
                    ).wait_recv()
                feat, norm = features(z, c)
                f_own[...] = feat
                n_own[...] = norm

            for xx in range(nx):
                e_wait(b, other, xx)

            @pl.loop(0, nc)
            def _(cc):
                feat, norm = features(b, cc)
                tile(b, cc, feat, norm)

    @pl.loop(0, nz + 2)
    def _(t):
        @pl.when(t < nz)
        def _():
            stage_z(t, 0)
            stage_z(t, 1)

        @pl.when(jnp.logical_and(t >= 1, t < nz + 1))
        def _():
            stage_x(t - 1, 0)
            stage_x(t - 1, 1)

        @pl.when(t >= 2)
        def _():
            stage_c(t - 2, 0)
            stage_c(t - 2, 1)

    own_weight = jnp.sum(jnp.where(eye(), weight_row(z, c), 0.0), axis=1, keepdims=True)
    grad = (
        own_weight * (accum[...] - f_own[...].astype(jnp.float32) * (2.0 * quot[...]))
    ).astype(jnp.bfloat16)
    f_own[...] = grad

    middle = nz // 2
    left_side = z < middle
    inward = jnp.where(left_side, z + 1, z - 1)
    outward = jnp.where(left_side, z - 1, z + 1)
    is_middle = jnp.logical_or(z == middle - 1, z == middle)
    is_outer = jnp.logical_or(z == 0, z == nz - 1)
    spot = is_middle.astype(jnp.int32)

    def hc_copy(k):
        return remote(
            h_core.at[k], h_recv.at[k], hc_send.at[k], hc_recv.at[k], {"rep": other}
        )

    def hi_copy(k):
        return remote(
            h_send.at[k], h_side.at[spot, k], hi_send.at[k], hi_recv.at[spot, k],
            {"loop": inward},
        )

    def hi_wait(place, k):
        remote(
            h_send.at[k], h_side.at[place, k], hi_send.at[k], hi_recv.at[place, k],
            {"loop": inward},
        ).wait_recv()

    def ho_copy(k):
        slot = h_full.at[c, k]
        return remote(slot, slot, ho_send.at[k], hf_recv.at[c, k], {"loop": outward})

    def hf_copy(k):
        slot = h_full.at[c, k]
        return remote(slot, slot, hf_send.at[k], hf_recv.at[c, k], {"rep": other})

    for k in range(PARTS):
        part = lax.dot_general(
            emb_ref[...], f_own[:, k * width : (k + 1) * width], (((0,), (0,)), ((), ())),
            preferred_element_type=jnp.float32,
        )
        h_full_part = part.reshape(nc, half, width)

        @pl.when(c == 0)
        def _():
            h_own[k] = h_full_part[0]
            h_core[k] = h_full_part[1].astype(jnp.bfloat16)

        @pl.when(c == 1)
        def _():
            h_own[k] = h_full_part[1]
            h_core[k] = h_full_part[0].astype(jnp.bfloat16)

        hc_copy(k).start()

    for k in range(PARTS):
        hc_copy(k).wait_recv()
        h_own[k] = h_own[k] + h_recv[k].astype(jnp.float32)

        @pl.when(is_outer)
        def _():
            h_send[k] = h_own[k].astype(jnp.bfloat16)
            hi_copy(k).start()

    for k in range(PARTS):
        @pl.when(jnp.logical_not(is_outer))
        def _():
            hi_wait(0, k)
            h_send[k] = (h_own[k] + h_side[0, k].astype(jnp.float32)).astype(jnp.bfloat16)
            hi_copy(k).start()

    embed_out[...] = lax.dot_general(
        f_own[...], head_ref[...], (((1,), (1,)), ((), ())), preferred_element_type=jnp.float32
    ).astype(jnp.bfloat16)

    for k in range(PARTS):
        @pl.when(is_middle)
        def _():
            hi_wait(1, k)
            h_full[c, k] = (
                h_send[k].astype(jnp.float32) + h_side[1, k].astype(jnp.float32)
            ).astype(jnp.bfloat16)

        @pl.when(jnp.logical_not(is_middle))
        def _():
            ho_copy(k).wait_recv()

        @pl.when(jnp.logical_not(is_outer))
        def _():
            ho_copy(k).start()

        hf_copy(k).start()

    for k in range(PARTS):
        head_out[pl.ds(pl.multiple_of(c * half, half), half), k * width : (k + 1) * width] = (
            h_full[c, k].astype(jnp.float32)
        )

    for k in range(PARTS):
        slot = h_full.at[other, k]
        remote(slot, slot, hf_send.at[k], hf_recv.at[other, k], {"rep": other}).wait_recv()
        head_out[pl.ds(pl.multiple_of(other * half, half), half), k * width : (k + 1) * width] = (
            h_full[other, k].astype(jnp.float32)
        )

    @pl.loop(0, nz)
    def _(b):
        @pl.when(jnp.logical_and(b <= z, has_right))
        def _():
            z_copy(b, 0).wait_send()

        @pl.when(jnp.logical_and(b >= z, has_left))
        def _():
            z_copy(b, 1).wait_send()

        @pl.when(b != pair)
        def _():
            for j in range(nx - 1):
                x_copy(b, j).wait_send()

        for xx in range(nx):
            c_copy(b, xx).wait_send()

    for j in range(nx - 1):
        zx_copy(j).wait_send()
        w_copy(j).wait_send()
        wc_copy(j).wait_send()
    for k in range(PARTS):
        hc_copy(k).wait_send()
        hi_copy(k).wait_send()
        hf_copy(k).wait_send()

        @pl.when(jnp.logical_not(is_outer))
        def _():
            ho_copy(k).wait_send()


def body(embeddings, head_weight, gp_weights, counts):
    nz, nx, nc = (lax.axis_size(name) for name in ("loop", "enc", "rep"))
    rows, cols = embeddings.shape
    feats = head_weight.shape[1]
    half, width = cols // nc, feats // PARTS
    gp_rows = gp_weights.reshape(nz * nc, rows)
    vmem = pl.BlockSpec(memory_space=pltpu.VMEM)
    dma = pltpu.SemaphoreType.DMA
    return pl.pallas_call(
        functools.partial(kernel, (nz, nx, nc)),
        out_shape=(
            jax.ShapeDtypeStruct((rows, cols), jnp.bfloat16),
            jax.ShapeDtypeStruct((cols, feats), jnp.float32),
        ),
        in_specs=[vmem, vmem, vmem, pl.BlockSpec(memory_space=pltpu.SMEM)],
        out_specs=(vmem, vmem),
        scratch_shapes=[
            pltpu.VMEM((nz, nc, nx, rows, cols), jnp.bfloat16),
            pltpu.VMEM((nx, nc, half, feats), jnp.bfloat16),
            pltpu.VMEM((rows, feats), jnp.bfloat16),
            pltpu.VMEM((rows, 1), jnp.float32),
            pltpu.VMEM((rows, feats), jnp.float32),
            pltpu.VMEM((rows, 1), jnp.float32),
            pltpu.VMEM((PARTS, half, width), jnp.float32),
            pltpu.VMEM((PARTS, half, width), jnp.bfloat16),
            pltpu.VMEM((PARTS, half, width), jnp.bfloat16),
            pltpu.VMEM((PARTS, half, width), jnp.bfloat16),
            pltpu.VMEM((2, PARTS, half, width), jnp.bfloat16),
            pltpu.VMEM((nc, PARTS, half, width), jnp.bfloat16),
            dma((nz, nc, nx)),
            dma((2, nz)),
            dma((nx - 1,)),
            dma((nx - 1, nz)),
            dma((nz, nx)),
            dma((nx - 1,)),
            dma((nx,)),
            dma((nx - 1,)),
            dma((nx - 1,)),
            dma((PARTS,)),
            dma((PARTS,)),
            dma((PARTS,)),
            dma((2, PARTS)),
            dma((PARTS,)),
            dma((PARTS,)),
            dma((nc, PARTS)),
        ],
        compiler_params=pltpu.CompilerParams(
            collective_id=0, has_side_effects=True, vmem_limit_bytes=56 * 1024 * 1024
        ),
    )(embeddings, head_weight, gp_rows, counts)


def solution(mesh):
    placed = (P(("groups", "loop", "rep"), "enc"), P("enc", None), P("groups"), P("groups"))
    return jax.shard_map(
        body,
        mesh=mesh,
        in_specs=placed,
        out_specs=(P(("groups", "loop", "rep"), "enc"), P(("groups", "enc"), None)),
        check_vma=False,
    )
```

```python
import functools

import jax
import jax.numpy as jnp
from jax import lax
from jax.experimental import pallas as pl
from jax.experimental.pallas import tpu as pltpu
from jax.sharding import PartitionSpec as P

EPSILON = 1e-06
PARTS = 6
CHUNKS = 2
MESH_ID = pl.DeviceIdType.MESH


def kernel(
    sizes,
    emb_ref,
    head_ref,
    gp_ref,
    counts_ref,
    embed_out,
    head_out,
    e_all,
    w_all,
    f_own,
    n_own,
    accum,
    quot,
    h_own,
    h_core,
    h_recv,
    h_send,
    h_side,
    h_full,
    e_recv,
    z_send,
    x_send,
    c_send,
    w_send,
    w_recv,
    wy_send,
    wc_send,
    wc_recv,
    in_sem,
    hc_send,
    hc_recv,
    hi_send,
    hi_recv,
    ho_send,
    hf_send,
    hf_recv,
):
    nz, nx, nc, ng = sizes
    z = lax.axis_index("loop")
    x = lax.axis_index("enc")
    c = lax.axis_index("rep")
    g = lax.axis_index("groups")
    other = 1 - c
    rows, cols = e_all.shape[3:]
    piece = rows // CHUNKS
    quarter, feats = w_all.shape[3:]
    half = quarter * ng
    width = feats // PARTS
    has_left = z > 0
    has_right = z < nz - 1

    def x_peer(j):
        return lax.rem(x + 1 + j, nx)

    def remote(src, dst, send, recv, device):
        return pltpu.make_async_remote_copy(
            src_ref=src, dst_ref=dst, send_sem=send, recv_sem=recv,
            device_id=device, device_id_type=MESH_ID,
        )

    def g_peer(i):
        return lax.rem(g + 1 + i, ng)

    def e_copy(b, cc, xx, h, send, device):
        start = h * piece if isinstance(h, int) else pl.multiple_of(h * piece, piece)
        slot = e_all.at[b, cc, xx, pl.ds(start, piece)]
        return remote(slot, slot, send, e_recv.at[b, cc, xx, h], device)

    def z_copy(b, d, h):
        return e_copy(b, c, x, h, z_send.at[d, b, h], {"loop": z + (1 if d == 0 else -1)})

    def x_copy(b, j, h):
        return e_copy(b, c, x, h, x_send.at[j, b, h], {"enc": x_peer(j)})

    def c_copy(b, xx, h):
        return e_copy(b, c, xx, h, c_send.at[b, xx, h], {"rep": other})

    def e_wait(b, cc, xx, h):
        e_copy(b, cc, xx, h, c_send.at[b, xx, h], {"rep": other}).wait_recv()

    def w_copy(xx, gg, send, device):
        slot = w_all.at[xx, c, gg]
        return remote(slot, slot, send, w_recv.at[xx, gg], device)

    def wx_copy(j):
        return w_copy(x, g, w_send.at[j], {"enc": x_peer(j)})

    def wy_copy(j, i):
        return w_copy(x_peer(j), g, wy_send.at[j, i], {"groups": g_peer(i)})

    def w_wait(xx, gg):
        w_copy(xx, gg, w_send.at[0], {"rep": other}).wait_recv()

    def wc_copy(xx, cc, gg):
        slot = w_all.at[xx, cc, gg]
        return remote(slot, slot, wc_send.at[xx, gg], wc_recv.at[xx, gg], {"rep": other})

    own_emb = pltpu.make_async_copy(emb_ref, e_all.at[z, c, x], in_sem.at[0])
    own_emb.start()
    own_head = []
    for cc in range(nc):
        for gg in range(ng):
            start = (cc * ng + gg) * quarter
            own_head.append(
                pltpu.make_async_copy(
                    head_ref.at[pl.ds(start, quarter)],
                    w_all.at[x, cc, gg],
                    in_sem.at[1 + cc * ng + gg],
                )
            )
            own_head[-1].start()

    barrier = pltpu.get_barrier_semaphore()

    @pl.when(has_left)
    def _():
        pl.semaphore_signal(barrier, 1, device_id={"loop": z - 1}, device_id_type=MESH_ID)

    @pl.when(has_right)
    def _():
        pl.semaphore_signal(barrier, 1, device_id={"loop": z + 1}, device_id_type=MESH_ID)

    for j in range(nx - 1):
        pl.semaphore_signal(barrier, 1, device_id={"enc": x_peer(j)}, device_id_type=MESH_ID)
    pl.semaphore_signal(barrier, 1, device_id={"rep": other}, device_id_type=MESH_ID)

    for i in range(ng - 1):
        pl.semaphore_signal(barrier, 1, device_id={"groups": g_peer(i)}, device_id_type=MESH_ID)
    accum[...] = jnp.zeros_like(accum)
    quot[...] = jnp.zeros_like(quot)

    pl.semaphore_wait(
        barrier, nx + ng - 1 + has_left.astype(jnp.int32) + has_right.astype(jnp.int32)
    )
    own_emb.wait()
    for copy in own_head:
        copy.wait()
    for j in range(nx - 1):
        wx_copy(j).start()

    def features(b, cc):
        total = jnp.dot(
            e_all[b, cc, 0], w_all[0].reshape(cols, feats),
            preferred_element_type=jnp.float32,
        )
        for xx in range(1, nx):
            total = total + jnp.dot(
                e_all[b, cc, xx], w_all[xx].reshape(cols, feats),
                preferred_element_type=jnp.float32,
            )
        total = total.astype(jnp.bfloat16)
        wide = total.astype(jnp.float32)
        return total, jnp.sum(wide * wide, axis=1, keepdims=True)

    def eye():
        return lax.broadcasted_iota(jnp.int32, (rows, rows), 0) == lax.broadcasted_iota(
            jnp.int32, (rows, rows), 1
        )

    def weight_row(b, cc):
        place = cc * rows + lax.broadcasted_iota(jnp.int32, (1, rows), 1)
        lanes = gp_ref.shape[1]
        split = rows // lanes
        first = (b * nc + cc) * split
        held = [gp_ref[pl.ds(first + i, 1), :] for i in range(split)]
        return jnp.where(place < counts_ref[b], jnp.concatenate(held, axis=1), 0.0)

    def tile(b, cc, feat, norm):
        norm_row = jnp.sum(jnp.where(eye(), norm, 0.0), axis=0, keepdims=True)
        scores = lax.dot_general(
            f_own[...], feat, (((1,), (1,)), ((), ())), preferred_element_type=jnp.float32
        )
        both = n_own[...] + norm_row
        denom = both - scores + EPSILON
        scaled = weight_row(b, cc) * (1.0 / (denom * denom))
        quot[...] += jnp.sum(scaled * scores, axis=1, keepdims=True)
        accum[...] += jnp.dot(
            (both * scaled).astype(jnp.bfloat16), feat, preferred_element_type=jnp.float32
        )

    def at_step(s, d):
        b = z - s if d == 0 else z + s
        return b, jnp.logical_and(jnp.logical_and(b >= 0, b < nz), s >= (1 if d else 0))

    def stage_z(u, d):
        s, h = u // CHUNKS, lax.rem(u, CHUNKS)
        b, valid = at_step(s, d)

        @pl.when(valid)
        def _():
            @pl.when(s > 0)
            def _():
                e_wait(b, c, x, h)

            @pl.when(has_right if d == 0 else has_left)
            def _():
                z_copy(b, d, h).start()

            if d == 0:
                @pl.when(jnp.logical_and(s == 0, has_left))
                def _():
                    z_copy(b, 1, h).start()

            for j in range(nx - 1):
                x_copy(b, j, h).start()
            c_copy(b, x, h).start()

    def stage_x(u, d):
        s, h = u // CHUNKS, lax.rem(u, CHUNKS)
        b, valid = at_step(s, d)

        @pl.when(valid)
        def _():
            for j in range(nx - 1):
                e_wait(b, c, x_peer(j), h)
                c_copy(b, x_peer(j), h).start()

    def stage_w():
        for j in range(nx - 1):
            w_wait(x_peer(j), g)
            for i in range(ng - 1):
                wy_copy(j, i).start()
            wc_copy(x_peer(j), c, g).start()

    def stage_first():
        for j in range(nx - 1):
            for i in range(ng - 1):
                w_wait(x_peer(j), g_peer(i))
                wc_copy(x_peer(j), c, g_peer(i)).start()
        for j in range(nx - 1):
            for gg in range(ng):
                wc_copy(x_peer(j), other, gg).wait_recv()
        feat, norm = features(z, c)
        f_own[...] = feat
        n_own[...] = norm

    def stage_c(s, d):
        b, valid = at_step(s, d)

        @pl.when(valid)
        def _():
            for h in range(CHUNKS):
                for xx in range(nx):
                    e_wait(b, other, xx, h)

            @pl.loop(0, nc)
            def _(cc):
                feat, norm = features(b, cc)
                tile(b, cc, feat, norm)

    steps = nz * CHUNKS
    x_lag = 3
    c_lag = 3 + CHUNKS

    @pl.loop(0, steps + c_lag - 1)
    def _(t):
        @pl.when(t < steps)
        def _():
            stage_z(t, 0)
            stage_z(t, 1)

        @pl.when(t == 2)
        def _():
            stage_w()

        @pl.when(t == c_lag)
        def _():
            stage_first()

        @pl.when(jnp.logical_and(t >= c_lag, lax.rem(t - c_lag + CHUNKS, CHUNKS) == 0))
        def _():
            stage_c((t - c_lag) // CHUNKS, 0)
            stage_c((t - c_lag) // CHUNKS, 1)

        @pl.when(jnp.logical_and(t >= x_lag, t < steps + x_lag))
        def _():
            stage_x(t - x_lag, 0)
            stage_x(t - x_lag, 1)

    own_weight = jnp.sum(jnp.where(eye(), weight_row(z, c), 0.0), axis=1, keepdims=True)
    grad = (
        own_weight * (accum[...] - f_own[...].astype(jnp.float32) * (2.0 * quot[...]))
    ).astype(jnp.bfloat16)
    f_own[...] = grad

    middle = nz // 2
    left_side = z < middle
    inward = jnp.where(left_side, z + 1, z - 1)
    outward = jnp.where(left_side, z - 1, z + 1)
    is_middle = jnp.logical_or(z == middle - 1, z == middle)
    is_outer = jnp.logical_or(z == 0, z == nz - 1)
    spot = is_middle.astype(jnp.int32)

    def hc_copy(k):
        return remote(
            h_core.at[k], h_recv.at[k], hc_send.at[k], hc_recv.at[k], {"rep": other}
        )

    def hi_copy(k):
        return remote(
            h_send.at[k], h_side.at[spot, k], hi_send.at[k], hi_recv.at[spot, k],
            {"loop": inward},
        )

    def hi_wait(place, k):
        remote(
            h_send.at[k], h_side.at[place, k], hi_send.at[k], hi_recv.at[place, k],
            {"loop": inward},
        ).wait_recv()

    def ho_copy(k):
        slot = h_full.at[c, k]
        return remote(slot, slot, ho_send.at[k], hf_recv.at[c, k], {"loop": outward})

    def hf_copy(k):
        slot = h_full.at[c, k]
        return remote(slot, slot, hf_send.at[k], hf_recv.at[c, k], {"rep": other})

    for k in range(PARTS):
        part = lax.dot_general(
            e_all[z, c, x], f_own[:, k * width : (k + 1) * width], (((0,), (0,)), ((), ())),
            preferred_element_type=jnp.float32,
        )
        h_full_part = part.reshape(nc, half, width)

        @pl.when(c == 0)
        def _():
            h_own[k] = h_full_part[0]
            h_core[k] = h_full_part[1].astype(jnp.bfloat16)

        @pl.when(c == 1)
        def _():
            h_own[k] = h_full_part[1]
            h_core[k] = h_full_part[0].astype(jnp.bfloat16)

        hc_copy(k).start()

    for k in range(PARTS):
        hc_copy(k).wait_recv()
        h_own[k] = h_own[k] + h_recv[k].astype(jnp.float32)

        @pl.when(is_outer)
        def _():
            h_send[k] = h_own[k].astype(jnp.bfloat16)
            hi_copy(k).start()

    for k in range(PARTS):
        @pl.when(jnp.logical_not(is_outer))
        def _():
            hi_wait(0, k)
            h_send[k] = (h_own[k] + h_side[0, k].astype(jnp.float32)).astype(jnp.bfloat16)
            hi_copy(k).start()

    embed_out[...] = lax.dot_general(
        f_own[...], w_all[x].reshape(cols, feats), (((1,), (1,)), ((), ())), preferred_element_type=jnp.float32
    ).astype(jnp.bfloat16)

    for k in range(PARTS):
        @pl.when(is_middle)
        def _():
            hi_wait(1, k)
            h_full[c, k] = (
                h_send[k].astype(jnp.float32) + h_side[1, k].astype(jnp.float32)
            ).astype(jnp.bfloat16)

        @pl.when(jnp.logical_not(is_middle))
        def _():
            ho_copy(k).wait_recv()

        @pl.when(jnp.logical_not(is_outer))
        def _():
            ho_copy(k).start()

        hf_copy(k).start()

    for k in range(PARTS):
        slot = h_full.at[other, k]
        remote(slot, slot, hf_send.at[k], hf_recv.at[other, k], {"rep": other}).wait_recv()
    head_out[...] = h_full[...]

    @pl.loop(0, nz)
    def _(b):
        for h in range(CHUNKS):
            @pl.when(jnp.logical_and(b <= z, has_right))
            def _():
                z_copy(b, 0, h).wait_send()

            @pl.when(jnp.logical_and(b >= z, has_left))
            def _():
                z_copy(b, 1, h).wait_send()

            for j in range(nx - 1):
                x_copy(b, j, h).wait_send()
            for xx in range(nx):
                c_copy(b, xx, h).wait_send()

    for j in range(nx - 1):
        wx_copy(j).wait_send()
        for i in range(ng - 1):
            wy_copy(j, i).wait_send()
        for gg in range(ng):
            wc_copy(x_peer(j), c, gg).wait_send()
    for k in range(PARTS):
        hc_copy(k).wait_send()
        hi_copy(k).wait_send()
        hf_copy(k).wait_send()

        @pl.when(jnp.logical_not(is_outer))
        def _():
            ho_copy(k).wait_send()


def finish(embed_ref, head_ref, embed_out, head_out):
    cores, parts, half, width = head_ref.shape
    embed_out[...] = embed_ref[...]
    for cc in range(cores):
        for k in range(parts):
            head_out[cc * half : (cc + 1) * half, k * width : (k + 1) * width] = head_ref[
                cc, k
            ].astype(jnp.float32)


def body(embeddings, head_weight, gp_weights, counts):
    nz, nx, nc, ng = (lax.axis_size(name) for name in ("loop", "enc", "rep", "groups"))
    rows, cols = embeddings.shape
    feats = head_weight.shape[1]
    half, width = cols // nc, feats // PARTS
    if half % (16 * ng):
        raise ValueError("head rows")
    gp_rows = gp_weights.reshape(-1, 128)
    vmem = pl.BlockSpec(memory_space=pltpu.VMEM)
    hbm = pl.BlockSpec(memory_space=pl.ANY)
    dma = pltpu.SemaphoreType.DMA
    held = 2 * (nz * nc * nx * rows * cols + nx * cols * feats)
    embed_grad, head_sum = pl.pallas_call(
        functools.partial(kernel, (nz, nx, nc, ng)),
        out_shape=(
            jax.ShapeDtypeStruct((rows, cols), jnp.bfloat16),
            jax.ShapeDtypeStruct((nc, PARTS, half, width), jnp.bfloat16),
        ),
        in_specs=[hbm, hbm, vmem, pl.BlockSpec(memory_space=pltpu.SMEM)],
        out_specs=(vmem, vmem),
        scratch_shapes=[
            pltpu.VMEM((nz, nc, nx, rows, cols), jnp.bfloat16),
            pltpu.VMEM((nx, nc, ng, half // ng, feats), jnp.bfloat16),
            pltpu.VMEM((rows, feats), jnp.bfloat16),
            pltpu.VMEM((rows, 1), jnp.float32),
            pltpu.VMEM((rows, feats), jnp.float32),
            pltpu.VMEM((rows, 1), jnp.float32),
            pltpu.VMEM((PARTS, half, width), jnp.float32),
            pltpu.VMEM((PARTS, half, width), jnp.bfloat16),
            pltpu.VMEM((PARTS, half, width), jnp.bfloat16),
            pltpu.VMEM((PARTS, half, width), jnp.bfloat16),
            pltpu.VMEM((2, PARTS, half, width), jnp.bfloat16),
            pltpu.VMEM((nc, PARTS, half, width), jnp.bfloat16),
            dma((nz, nc, nx, CHUNKS)),
            dma((2, nz, CHUNKS)),
            dma((nx - 1, nz, CHUNKS)),
            dma((nz, nx, CHUNKS)),
            dma((nx - 1,)),
            dma((nx, ng)),
            dma((nx - 1, max(ng - 1, 1))),
            dma((nx, ng)),
            dma((nx, ng)),
            dma((1 + nc * ng,)),
            dma((PARTS,)),
            dma((PARTS,)),
            dma((PARTS,)),
            dma((2, PARTS)),
            dma((PARTS,)),
            dma((PARTS,)),
            dma((nc, PARTS)),
        ],
        compiler_params=pltpu.CompilerParams(
            collective_id=0, has_side_effects=True, vmem_limit_bytes=held + 20 * 1024 * 1024
        ),
    )(embeddings, head_weight, gp_rows, counts)
    return pl.pallas_call(
        finish,
        out_shape=(
            jax.ShapeDtypeStruct((rows, cols), jnp.bfloat16),
            jax.ShapeDtypeStruct((cols, feats), jnp.float32),
        ),
        in_specs=[vmem, vmem],
        out_specs=(vmem, vmem),
        compiler_params=pltpu.CompilerParams(vmem_limit_bytes=12 * 1024 * 1024),
    )(embed_grad, head_sum)


def solution(mesh):
    placed = (P(("groups", "loop", "rep"), "enc"), P("enc", None), P("groups"), P("groups"))
    return jax.shard_map(
        body,
        mesh=mesh,
        in_specs=placed,
        out_specs=(P(("groups", "loop", "rep"), "enc"), P(("groups", "enc"), None)),
        check_vma=False,
    )
```

```python
import functools

import jax
import jax.numpy as jnp
from jax import lax
from jax.experimental import pallas as pl
from jax.experimental.pallas import tpu as pltpu
from jax.sharding import PartitionSpec as P

EPSILON = 1e-06
PARTS = 6
CHUNKS = 2
VMEM_BYTES = 60 * 1024 * 1024
MESH_ID = pl.DeviceIdType.MESH


def kernel(
    sizes,
    emb_ref,
    head_ref,
    gp_hbm,
    counts_hbm,
    embed_out,
    head_out,
    gp_ref,
    counts_ref,
    e_all,
    w_all,
    f_own,
    n_own,
    accum,
    quot,
    h_own,
    h_core,
    h_recv,
    h_send,
    h_side,
    h_full,
    e_recv,
    z_send,
    x_send,
    c_send,
    w_send,
    w_recv,
    wy_send,
    wc_send,
    wc_recv,
    in_sem,
    hc_send,
    hc_recv,
    hi_send,
    hi_recv,
    ho_send,
    hf_send,
    hf_recv,
):
    nz, nx, nc, ng = sizes
    z = lax.axis_index("loop")
    x = lax.axis_index("enc")
    c = lax.axis_index("rep")
    g = lax.axis_index("groups")
    other = 1 - c
    rows, cols = e_all.shape[3:]
    piece = rows // CHUNKS
    quarter, feats = w_all.shape[3:]
    half = quarter * ng
    width = feats // PARTS
    has_left = z > 0
    has_right = z < nz - 1

    def x_peer(j):
        return lax.rem(x + 1 + j, nx)

    def remote(src, dst, send, recv, device):
        return pltpu.make_async_remote_copy(
            src_ref=src, dst_ref=dst, send_sem=send, recv_sem=recv,
            device_id=device, device_id_type=MESH_ID,
        )

    def g_peer(i):
        return lax.rem(g + 1 + i, ng)

    def e_copy(b, cc, xx, h, send, device):
        start = h * piece if isinstance(h, int) else pl.multiple_of(h * piece, piece)
        slot = e_all.at[b, cc, xx, pl.ds(start, piece)]
        return remote(slot, slot, send, e_recv.at[b, cc, xx, h], device)

    def z_copy(b, d, h):
        return e_copy(b, c, x, h, z_send.at[d, b, h], {"loop": z + (1 if d == 0 else -1)})

    def x_copy(b, j, h):
        return e_copy(b, c, x, h, x_send.at[j, b, h], {"enc": x_peer(j)})

    def c_copy(b, xx, h):
        return e_copy(b, c, xx, h, c_send.at[b, xx, h], {"rep": other})

    def e_wait(b, cc, xx, h):
        e_copy(b, cc, xx, h, c_send.at[b, xx, h], {"rep": other}).wait_recv()

    def w_copy(xx, gg, send, device):
        slot = w_all.at[xx, c, gg]
        return remote(slot, slot, send, w_recv.at[xx, gg], device)

    def wx_copy(j):
        return w_copy(x, g, w_send.at[j], {"enc": x_peer(j)})

    def wy_copy(j, i):
        return w_copy(x_peer(j), g, wy_send.at[j, i], {"groups": g_peer(i)})

    def w_wait(xx, gg):
        w_copy(xx, gg, w_send.at[0], {"rep": other}).wait_recv()

    def wc_copy(xx, cc, gg):
        slot = w_all.at[xx, cc, gg]
        return remote(slot, slot, wc_send.at[xx, gg], wc_recv.at[xx, gg], {"rep": other})

    own_emb = pltpu.make_async_copy(emb_ref, e_all.at[z, c, x], in_sem.at[0])
    own_emb.start()
    own_head = [
        pltpu.make_async_copy(gp_hbm, gp_ref, in_sem.at[1]),
        pltpu.make_async_copy(counts_hbm, counts_ref, in_sem.at[2]),
    ]
    for copy in own_head:
        copy.start()
    for cc in range(nc):
        for gg in range(ng):
            start = (cc * ng + gg) * quarter
            own_head.append(
                pltpu.make_async_copy(
                    head_ref.at[pl.ds(start, quarter)],
                    w_all.at[x, cc, gg],
                    in_sem.at[3 + cc * ng + gg],
                )
            )
            own_head[-1].start()

    barrier = pltpu.get_barrier_semaphore()

    @pl.when(has_left)
    def _():
        pl.semaphore_signal(barrier, 1, device_id={"loop": z - 1}, device_id_type=MESH_ID)

    @pl.when(has_right)
    def _():
        pl.semaphore_signal(barrier, 1, device_id={"loop": z + 1}, device_id_type=MESH_ID)

    for j in range(nx - 1):
        pl.semaphore_signal(barrier, 1, device_id={"enc": x_peer(j)}, device_id_type=MESH_ID)
    pl.semaphore_signal(barrier, 1, device_id={"rep": other}, device_id_type=MESH_ID)

    for i in range(ng - 1):
        pl.semaphore_signal(barrier, 1, device_id={"groups": g_peer(i)}, device_id_type=MESH_ID)
    accum[...] = jnp.zeros_like(accum)
    quot[...] = jnp.zeros_like(quot)

    pl.semaphore_wait(
        barrier, nx + ng - 1 + has_left.astype(jnp.int32) + has_right.astype(jnp.int32)
    )
    own_emb.wait()
    for copy in own_head:
        copy.wait()
    for j in range(nx - 1):
        wx_copy(j).start()

    def features(b, cc):
        total = jnp.dot(
            e_all[b, cc, 0], w_all[0].reshape(cols, feats),
            preferred_element_type=jnp.float32,
        )
        for xx in range(1, nx):
            total = total + jnp.dot(
                e_all[b, cc, xx], w_all[xx].reshape(cols, feats),
                preferred_element_type=jnp.float32,
            )
        total = total.astype(jnp.bfloat16)
        wide = total.astype(jnp.float32)
        return total, jnp.sum(wide * wide, axis=1, keepdims=True)

    def eye():
        return lax.broadcasted_iota(jnp.int32, (rows, rows), 0) == lax.broadcasted_iota(
            jnp.int32, (rows, rows), 1
        )

    def weight_row(b, cc):
        place = cc * rows + lax.broadcasted_iota(jnp.int32, (1, rows), 1)
        lanes = gp_ref.shape[1]
        split = rows // lanes
        first = (b * nc + cc) * split
        held = [gp_ref[pl.ds(first + i, 1), :] for i in range(split)]
        return jnp.where(place < counts_ref[b], jnp.concatenate(held, axis=1), 0.0)

    def tile(b, cc, feat, norm):
        norm_row = jnp.sum(jnp.where(eye(), norm, 0.0), axis=0, keepdims=True)
        scores = lax.dot_general(
            f_own[...], feat, (((1,), (1,)), ((), ())), preferred_element_type=jnp.float32
        )
        both = n_own[...] + norm_row
        denom = both - scores + EPSILON
        scaled = weight_row(b, cc) * (1.0 / (denom * denom))
        quot[...] += jnp.sum(scaled * scores, axis=1, keepdims=True)
        accum[...] += jnp.dot(
            (both * scaled).astype(jnp.bfloat16), feat, preferred_element_type=jnp.float32
        )

    def at_step(s, d):
        b = z - s if d == 0 else z + s
        return b, jnp.logical_and(jnp.logical_and(b >= 0, b < nz), s >= (1 if d else 0))

    def stage_z(u, d):
        s, h = u // CHUNKS, lax.rem(u, CHUNKS)
        b, valid = at_step(s, d)

        @pl.when(valid)
        def _():
            @pl.when(s > 0)
            def _():
                e_wait(b, c, x, h)

            @pl.when(has_right if d == 0 else has_left)
            def _():
                z_copy(b, d, h).start()

            if d == 0:
                @pl.when(jnp.logical_and(s == 0, has_left))
                def _():
                    z_copy(b, 1, h).start()

            for j in range(nx - 1):
                x_copy(b, j, h).start()
            c_copy(b, x, h).start()

    def stage_x(u, d):
        s, h = u // CHUNKS, lax.rem(u, CHUNKS)
        b, valid = at_step(s, d)

        @pl.when(valid)
        def _():
            for j in range(nx - 1):
                e_wait(b, c, x_peer(j), h)
                c_copy(b, x_peer(j), h).start()

    def stage_w():
        for j in range(nx - 1):
            w_wait(x_peer(j), g)
            for i in range(ng - 1):
                wy_copy(j, i).start()
            wc_copy(x_peer(j), c, g).start()

    def stage_first():
        for j in range(nx - 1):
            for i in range(ng - 1):
                w_wait(x_peer(j), g_peer(i))
                wc_copy(x_peer(j), c, g_peer(i)).start()
        for j in range(nx - 1):
            for gg in range(ng):
                wc_copy(x_peer(j), other, gg).wait_recv()
        feat, norm = features(z, c)
        f_own[...] = feat
        n_own[...] = norm

    def stage_c(s, d):
        b, valid = at_step(s, d)

        @pl.when(valid)
        def _():
            for h in range(CHUNKS):
                for xx in range(nx):
                    e_wait(b, other, xx, h)

            @pl.loop(0, nc)
            def _(cc):
                feat, norm = features(b, cc)
                tile(b, cc, feat, norm)

    steps = nz * CHUNKS
    x_lag = 3
    c_lag = 3 + CHUNKS

    @pl.loop(0, steps + c_lag - 1)
    def _(t):
        @pl.when(t < steps)
        def _():
            stage_z(t, 0)
            stage_z(t, 1)

        @pl.when(t == 2)
        def _():
            stage_w()

        @pl.when(t == c_lag)
        def _():
            stage_first()

        @pl.when(jnp.logical_and(t >= c_lag, lax.rem(t - c_lag + CHUNKS, CHUNKS) == 0))
        def _():
            stage_c((t - c_lag) // CHUNKS, 0)
            stage_c((t - c_lag) // CHUNKS, 1)

        @pl.when(jnp.logical_and(t >= x_lag, t < steps + x_lag))
        def _():
            stage_x(t - x_lag, 0)
            stage_x(t - x_lag, 1)

    own_weight = jnp.sum(jnp.where(eye(), weight_row(z, c), 0.0), axis=1, keepdims=True)
    grad = (
        own_weight * (accum[...] - f_own[...].astype(jnp.float32) * (2.0 * quot[...]))
    ).astype(jnp.bfloat16)
    f_own[...] = grad

    middle = nz // 2
    left_side = z < middle
    inward = jnp.where(left_side, z + 1, z - 1)
    outward = jnp.where(left_side, z - 1, z + 1)
    is_middle = jnp.logical_or(z == middle - 1, z == middle)
    is_outer = jnp.logical_or(z == 0, z == nz - 1)
    spot = is_middle.astype(jnp.int32)

    def hc_copy(k):
        return remote(
            h_core.at[k], h_recv.at[k], hc_send.at[k], hc_recv.at[k], {"rep": other}
        )

    def hi_copy(k):
        return remote(
            h_send.at[k], h_side.at[spot, k], hi_send.at[k], hi_recv.at[spot, k],
            {"loop": inward},
        )

    def hi_wait(place, k):
        remote(
            h_send.at[k], h_side.at[place, k], hi_send.at[k], hi_recv.at[place, k],
            {"loop": inward},
        ).wait_recv()

    def ho_copy(k):
        slot = h_full.at[c, k]
        return remote(slot, slot, ho_send.at[k], hf_recv.at[c, k], {"loop": outward})

    def hf_copy(k):
        slot = h_full.at[c, k]
        return remote(slot, slot, hf_send.at[k], hf_recv.at[c, k], {"rep": other})

    for k in range(PARTS):
        part = lax.dot_general(
            e_all[z, c, x], f_own[:, k * width : (k + 1) * width], (((0,), (0,)), ((), ())),
            preferred_element_type=jnp.float32,
        )
        h_full_part = part.reshape(nc, half, width)

        @pl.when(c == 0)
        def _():
            h_own[k] = h_full_part[0]
            h_core[k] = h_full_part[1].astype(jnp.bfloat16)

        @pl.when(c == 1)
        def _():
            h_own[k] = h_full_part[1]
            h_core[k] = h_full_part[0].astype(jnp.bfloat16)

        hc_copy(k).start()

    for k in range(PARTS):
        hc_copy(k).wait_recv()
        h_own[k] = h_own[k] + h_recv[k].astype(jnp.float32)

        @pl.when(is_outer)
        def _():
            h_send[k] = h_own[k].astype(jnp.bfloat16)
            hi_copy(k).start()

    for k in range(PARTS):
        @pl.when(jnp.logical_not(is_outer))
        def _():
            hi_wait(0, k)
            h_send[k] = (h_own[k] + h_side[0, k].astype(jnp.float32)).astype(jnp.bfloat16)
            hi_copy(k).start()

    embed_out[...] = lax.dot_general(
        f_own[...], w_all[x].reshape(cols, feats), (((1,), (1,)), ((), ())), preferred_element_type=jnp.float32
    ).astype(jnp.bfloat16)

    for k in range(PARTS):
        @pl.when(is_middle)
        def _():
            hi_wait(1, k)
            h_full[c, k] = (
                h_send[k].astype(jnp.float32) + h_side[1, k].astype(jnp.float32)
            ).astype(jnp.bfloat16)

        @pl.when(jnp.logical_not(is_middle))
        def _():
            ho_copy(k).wait_recv()

        @pl.when(jnp.logical_not(is_outer))
        def _():
            ho_copy(k).start()

        hf_copy(k).start()

    for k in range(PARTS):
        slot = h_full.at[other, k]
        remote(slot, slot, hf_send.at[k], hf_recv.at[other, k], {"rep": other}).wait_recv()
    head_out[...] = h_full[...]

    @pl.loop(0, nz)
    def _(b):
        for h in range(CHUNKS):
            @pl.when(jnp.logical_and(b <= z, has_right))
            def _():
                z_copy(b, 0, h).wait_send()

            @pl.when(jnp.logical_and(b >= z, has_left))
            def _():
                z_copy(b, 1, h).wait_send()

            for j in range(nx - 1):
                x_copy(b, j, h).wait_send()
            for xx in range(nx):
                c_copy(b, xx, h).wait_send()

    for j in range(nx - 1):
        wx_copy(j).wait_send()
        for i in range(ng - 1):
            wy_copy(j, i).wait_send()
        for gg in range(ng):
            wc_copy(x_peer(j), c, gg).wait_send()
    for k in range(PARTS):
        hc_copy(k).wait_send()
        hi_copy(k).wait_send()
        hf_copy(k).wait_send()

        @pl.when(jnp.logical_not(is_outer))
        def _():
            ho_copy(k).wait_send()


def finish(embed_ref, head_ref, embed_out, head_out):
    cores, parts, half, width = head_ref.shape
    embed_out[...] = embed_ref[...]
    for cc in range(cores):
        for k in range(parts):
            head_out[cc * half : (cc + 1) * half, k * width : (k + 1) * width] = head_ref[
                cc, k
            ].astype(jnp.float32)


def body(embeddings, head_weight, gp_weights, counts):
    nz, nx, nc, ng = (lax.axis_size(name) for name in ("loop", "enc", "rep", "groups"))
    rows, cols = embeddings.shape
    feats = head_weight.shape[1]
    half, width = cols // nc, feats // PARTS
    if half % (16 * ng):
        raise ValueError("head rows")
    gp_rows = gp_weights.reshape(-1, 128)
    vmem = pl.BlockSpec(memory_space=pltpu.VMEM)
    hbm = pl.BlockSpec(memory_space=pltpu.HBM)
    dma = pltpu.SemaphoreType.DMA
    embed_grad, head_sum = pl.pallas_call(
        functools.partial(kernel, (nz, nx, nc, ng)),
        out_shape=(
            jax.ShapeDtypeStruct((rows, cols), jnp.bfloat16),
            jax.ShapeDtypeStruct((nc, PARTS, half, width), jnp.bfloat16),
        ),
        in_specs=[hbm, hbm, hbm, hbm],
        out_specs=(vmem, vmem),
        scratch_shapes=[
            pltpu.VMEM(gp_rows.shape, jnp.float32),
            pltpu.SMEM(counts.shape, jnp.int32),
            pltpu.VMEM((nz, nc, nx, rows, cols), jnp.bfloat16),
            pltpu.VMEM((nx, nc, ng, half // ng, feats), jnp.bfloat16),
            pltpu.VMEM((rows, feats), jnp.bfloat16),
            pltpu.VMEM((rows, 1), jnp.float32),
            pltpu.VMEM((rows, feats), jnp.float32),
            pltpu.VMEM((rows, 1), jnp.float32),
            pltpu.VMEM((PARTS, half, width), jnp.float32),
            pltpu.VMEM((PARTS, half, width), jnp.bfloat16),
            pltpu.VMEM((PARTS, half, width), jnp.bfloat16),
            pltpu.VMEM((PARTS, half, width), jnp.bfloat16),
            pltpu.VMEM((2, PARTS, half, width), jnp.bfloat16),
            pltpu.VMEM((nc, PARTS, half, width), jnp.bfloat16),
            dma((nz, nc, nx, CHUNKS)),
            dma((2, nz, CHUNKS)),
            dma((nx - 1, nz, CHUNKS)),
            dma((nz, nx, CHUNKS)),
            dma((nx - 1,)),
            dma((nx, ng)),
            dma((nx - 1, max(ng - 1, 1))),
            dma((nx, ng)),
            dma((nx, ng)),
            dma((3 + nc * ng,)),
            dma((PARTS,)),
            dma((PARTS,)),
            dma((PARTS,)),
            dma((2, PARTS)),
            dma((PARTS,)),
            dma((PARTS,)),
            dma((nc, PARTS)),
        ],
        compiler_params=pltpu.CompilerParams(
            collective_id=0, has_side_effects=True, vmem_limit_bytes=VMEM_BYTES
        ),
    )(embeddings, head_weight, gp_rows, counts)
    return pl.pallas_call(
        finish,
        out_shape=(
            jax.ShapeDtypeStruct((rows, cols), jnp.bfloat16),
            jax.ShapeDtypeStruct((cols, feats), jnp.float32),
        ),
        in_specs=[vmem, vmem],
        out_specs=(vmem, vmem),
        compiler_params=pltpu.CompilerParams(vmem_limit_bytes=12 * 1024 * 1024),
    )(embed_grad, head_sum)


def solution(mesh):
    placed = (P(("groups", "loop", "rep"), "enc"), P("enc", None), P("groups"), P("groups"))
    return jax.shard_map(
        body,
        mesh=mesh,
        in_specs=placed,
        out_specs=(P(("groups", "loop", "rep"), "enc"), P(("groups", "enc"), None)),
        check_vma=False,
    )
```

```python
import functools

import jax
import jax.numpy as jnp
from jax import lax
from jax.experimental import pallas as pl
from jax.experimental.pallas import tpu as pltpu
from jax.sharding import PartitionSpec as P

EPSILON = 1e-06
PARTS = 6
CHUNKS = 2
VMEM_BYTES = 60 * 1024 * 1024
MESH_ID = pl.DeviceIdType.MESH


def kernel(
    sizes,
    emb_ref,
    head_ref,
    gp_hbm,
    counts_hbm,
    embed_out,
    head_out,
    gp_ref,
    counts_ref,
    e_all,
    w_all,
    f_own,
    n_own,
    accum,
    quot,
    h_own,
    h_core,
    h_recv,
    h_send,
    h_side,
    h_full,
    e_recv,
    z_send,
    x_send,
    c_send,
    w_send,
    w_recv,
    wy_send,
    wc_send,
    wc_recv,
    in_sem,
    hc_send,
    hc_recv,
    hi_send,
    hi_recv,
    ho_send,
    hf_send,
    hf_recv,
):
    nz, nx, nc, ng = sizes
    z = lax.axis_index("loop")
    x = lax.axis_index("enc")
    c = lax.axis_index("rep")
    g = lax.axis_index("groups")
    other = 1 - c
    rows, cols = e_all.shape[3:]
    piece = rows // CHUNKS
    quarter, feats = w_all.shape[3:]
    half = quarter * ng
    width = feats // PARTS
    has_left = z > 0
    has_right = z < nz - 1

    def x_peer(j):
        return lax.rem(x + 1 + j, nx)

    def remote(src, dst, send, recv, device):
        return pltpu.make_async_remote_copy(
            src_ref=src, dst_ref=dst, send_sem=send, recv_sem=recv,
            device_id=device, device_id_type=MESH_ID,
        )

    def g_peer(i):
        return lax.rem(g + 1 + i, ng)

    def e_copy(b, cc, xx, h, send, device):
        start = h * piece if isinstance(h, int) else pl.multiple_of(h * piece, piece)
        slot = e_all.at[b, cc, xx, pl.ds(start, piece)]
        return remote(slot, slot, send, e_recv.at[b, cc, xx, h], device)

    def z_copy(b, d, h):
        return e_copy(b, c, x, h, z_send.at[d, b, h], {"loop": z + (1 if d == 0 else -1)})

    def x_copy(b, j, h):
        return e_copy(b, c, x, h, x_send.at[j, b, h], {"enc": x_peer(j)})

    def c_copy(b, xx, h):
        return e_copy(b, c, xx, h, c_send.at[b, xx, h], {"rep": other})

    def e_wait(b, cc, xx, h):
        e_copy(b, cc, xx, h, c_send.at[b, xx, h], {"rep": other}).wait_recv()

    def w_copy(xx, gg, send, device):
        slot = w_all.at[xx, c, gg]
        return remote(slot, slot, send, w_recv.at[xx, gg], device)

    def wx_copy(j):
        return w_copy(x, g, w_send.at[j], {"enc": x_peer(j)})

    def wy_copy(j, i):
        return w_copy(x_peer(j), g, wy_send.at[j, i], {"groups": g_peer(i)})

    def w_wait(xx, gg):
        w_copy(xx, gg, w_send.at[0], {"rep": other}).wait_recv()

    def wc_copy(xx, cc, gg):
        slot = w_all.at[xx, cc, gg]
        return remote(slot, slot, wc_send.at[xx, gg], wc_recv.at[xx, gg], {"rep": other})

    own_emb = pltpu.make_async_copy(emb_ref, e_all.at[z, c, x], in_sem.at[0])
    own_emb.start()
    own_head = [
        pltpu.make_async_copy(gp_hbm, gp_ref, in_sem.at[1]),
        pltpu.make_async_copy(counts_hbm, counts_ref, in_sem.at[2]),
    ]
    for copy in own_head:
        copy.start()
    for cc in range(nc):
        for gg in range(ng):
            start = (cc * ng + gg) * quarter
            own_head.append(
                pltpu.make_async_copy(
                    head_ref.at[pl.ds(start, quarter)],
                    w_all.at[x, cc, gg],
                    in_sem.at[3 + cc * ng + gg],
                )
            )
            own_head[-1].start()

    barrier = pltpu.get_barrier_semaphore()

    @pl.when(has_left)
    def _():
        pl.semaphore_signal(barrier, 1, device_id={"loop": z - 1}, device_id_type=MESH_ID)

    @pl.when(has_right)
    def _():
        pl.semaphore_signal(barrier, 1, device_id={"loop": z + 1}, device_id_type=MESH_ID)

    for j in range(nx - 1):
        pl.semaphore_signal(barrier, 1, device_id={"enc": x_peer(j)}, device_id_type=MESH_ID)
    pl.semaphore_signal(barrier, 1, device_id={"rep": other}, device_id_type=MESH_ID)

    for i in range(ng - 1):
        pl.semaphore_signal(barrier, 1, device_id={"groups": g_peer(i)}, device_id_type=MESH_ID)
    accum[...] = jnp.zeros_like(accum)
    quot[...] = jnp.zeros_like(quot)

    pl.semaphore_wait(
        barrier, nx + ng - 1 + has_left.astype(jnp.int32) + has_right.astype(jnp.int32)
    )
    own_emb.wait()
    for copy in own_head:
        copy.wait()
    for j in range(nx - 1):
        wx_copy(j).start()

    def features(b, cc):
        total = jnp.dot(
            e_all[b, cc, 0], w_all[0].reshape(cols, feats),
            preferred_element_type=jnp.float32,
        )
        for xx in range(1, nx):
            total = total + jnp.dot(
                e_all[b, cc, xx], w_all[xx].reshape(cols, feats),
                preferred_element_type=jnp.float32,
            )
        total = total.astype(jnp.bfloat16)
        wide = total.astype(jnp.float32)
        return total, jnp.sum(wide * wide, axis=1, keepdims=True)

    def eye():
        return lax.broadcasted_iota(jnp.int32, (rows, rows), 0) == lax.broadcasted_iota(
            jnp.int32, (rows, rows), 1
        )

    def weight_row(b, cc):
        place = cc * rows + lax.broadcasted_iota(jnp.int32, (1, rows), 1)
        lanes = gp_ref.shape[1]
        split = rows // lanes
        first = (b * nc + cc) * split
        held = [gp_ref[pl.ds(first + i, 1), :] for i in range(split)]
        return jnp.where(place < counts_ref[b], jnp.concatenate(held, axis=1), 0.0)

    def tile(b, cc, feat, norm):
        norm_row = jnp.sum(jnp.where(eye(), norm, 0.0), axis=0, keepdims=True)
        scores = lax.dot_general(
            f_own[...], feat, (((1,), (1,)), ((), ())), preferred_element_type=jnp.float32
        )
        both = n_own[...] + norm_row
        denom = both - scores + EPSILON
        scaled = weight_row(b, cc) * (1.0 / (denom * denom))
        quot[...] += jnp.sum(scaled * scores, axis=1, keepdims=True)
        accum[...] += jnp.dot(
            (both * scaled).astype(jnp.bfloat16), feat, preferred_element_type=jnp.float32
        )

    def at_step(s, d):
        b = z - s if d == 0 else z + s
        return b, jnp.logical_and(jnp.logical_and(b >= 0, b < nz), s >= (1 if d else 0))

    def stage_z(u, d):
        s, h = u // CHUNKS, lax.rem(u, CHUNKS)
        b, valid = at_step(s, d)

        @pl.when(valid)
        def _():
            @pl.when(s > 0)
            def _():
                e_wait(b, c, x, h)

            @pl.when(has_right if d == 0 else has_left)
            def _():
                z_copy(b, d, h).start()

            if d == 0:
                @pl.when(jnp.logical_and(s == 0, has_left))
                def _():
                    z_copy(b, 1, h).start()

            for j in range(nx - 1):
                x_copy(b, j, h).start()
            c_copy(b, x, h).start()

    def stage_x(u, d):
        s, h = u // CHUNKS, lax.rem(u, CHUNKS)
        b, valid = at_step(s, d)

        @pl.when(valid)
        def _():
            for j in range(nx - 1):
                e_wait(b, c, x_peer(j), h)
                c_copy(b, x_peer(j), h).start()

    def stage_w():
        for j in range(nx - 1):
            w_wait(x_peer(j), g)
            for i in range(ng - 1):
                wy_copy(j, i).start()
            wc_copy(x_peer(j), c, g).start()

    def stage_first():
        for j in range(nx - 1):
            for i in range(ng - 1):
                w_wait(x_peer(j), g_peer(i))
                wc_copy(x_peer(j), c, g_peer(i)).start()
        for j in range(nx - 1):
            for gg in range(ng):
                wc_copy(x_peer(j), other, gg).wait_recv()
        feat, norm = features(z, c)
        f_own[...] = feat
        n_own[...] = norm

    def stage_c(s, d):
        b, valid = at_step(s, d)

        @pl.when(valid)
        def _():
            for h in range(CHUNKS):
                for xx in range(nx):
                    e_wait(b, other, xx, h)

            @pl.loop(0, nc)
            def _(cc):
                feat, norm = features(b, cc)
                tile(b, cc, feat, norm)

    steps = nz * CHUNKS
    x_lag = 3
    c_lag = 3 + CHUNKS

    @pl.loop(0, steps + c_lag - 1)
    def _(t):
        @pl.when(t < steps)
        def _():
            stage_z(t, 0)
            stage_z(t, 1)

        @pl.when(t == 2)
        def _():
            stage_w()

        @pl.when(t == c_lag)
        def _():
            stage_first()

        @pl.when(jnp.logical_and(t >= c_lag, lax.rem(t - c_lag + CHUNKS, CHUNKS) == 0))
        def _():
            stage_c((t - c_lag) // CHUNKS, 0)
            stage_c((t - c_lag) // CHUNKS, 1)

        @pl.when(jnp.logical_and(t >= x_lag, t < steps + x_lag))
        def _():
            stage_x(t - x_lag, 0)
            stage_x(t - x_lag, 1)

    own_weight = jnp.sum(jnp.where(eye(), weight_row(z, c), 0.0), axis=1, keepdims=True)
    grad = (
        own_weight * (accum[...] - f_own[...].astype(jnp.float32) * (2.0 * quot[...]))
    ).astype(jnp.bfloat16)
    f_own[...] = grad

    middle = nz // 2
    left_side = z < middle
    inward = jnp.where(left_side, z + 1, z - 1)
    outward = jnp.where(left_side, z - 1, z + 1)
    is_middle = jnp.logical_or(z == middle - 1, z == middle)
    is_outer = jnp.logical_or(z == 0, z == nz - 1)
    spot = is_middle.astype(jnp.int32)

    def hc_copy(k):
        return remote(
            h_core.at[k], h_recv.at[k], hc_send.at[k], hc_recv.at[k], {"rep": other}
        )

    def hi_copy(k):
        return remote(
            h_send.at[k], h_side.at[spot, k], hi_send.at[k], hi_recv.at[spot, k],
            {"loop": inward},
        )

    def hi_wait(place, k):
        remote(
            h_send.at[k], h_side.at[place, k], hi_send.at[k], hi_recv.at[place, k],
            {"loop": inward},
        ).wait_recv()

    def ho_copy(k):
        slot = h_full.at[c, k]
        return remote(slot, slot, ho_send.at[k], hf_recv.at[c, k], {"loop": outward})

    def hf_copy(k):
        slot = h_full.at[c, k]
        return remote(slot, slot, hf_send.at[k], hf_recv.at[c, k], {"rep": other})

    for k in range(PARTS):
        part = lax.dot_general(
            e_all[z, c, x], f_own[:, k * width : (k + 1) * width], (((0,), (0,)), ((), ())),
            preferred_element_type=jnp.float32,
        )
        h_full_part = part.reshape(nc, half, width)

        @pl.when(c == 0)
        def _():
            h_own[k] = h_full_part[0]
            h_core[k] = h_full_part[1].astype(jnp.bfloat16)

        @pl.when(c == 1)
        def _():
            h_own[k] = h_full_part[1]
            h_core[k] = h_full_part[0].astype(jnp.bfloat16)

        hc_copy(k).start()

    for k in range(PARTS):
        hc_copy(k).wait_recv()
        h_own[k] = h_own[k] + h_recv[k].astype(jnp.float32)

        @pl.when(is_outer)
        def _():
            h_send[k] = h_own[k].astype(jnp.bfloat16)
            hi_copy(k).start()

    for k in range(PARTS):
        @pl.when(jnp.logical_not(is_outer))
        def _():
            hi_wait(0, k)
            h_send[k] = (h_own[k] + h_side[0, k].astype(jnp.float32)).astype(jnp.bfloat16)
            hi_copy(k).start()

    embed_out[...] = lax.dot_general(
        f_own[...], w_all[x].reshape(cols, feats), (((1,), (1,)), ((), ())), preferred_element_type=jnp.float32
    ).astype(jnp.bfloat16)

    for k in range(PARTS):
        @pl.when(is_middle)
        def _():
            hi_wait(1, k)
            h_full[c, k] = (
                h_send[k].astype(jnp.float32) + h_side[1, k].astype(jnp.float32)
            ).astype(jnp.bfloat16)

        @pl.when(jnp.logical_not(is_middle))
        def _():
            ho_copy(k).wait_recv()

        @pl.when(jnp.logical_not(is_outer))
        def _():
            ho_copy(k).start()

        hf_copy(k).start()

    for k in range(PARTS):
        slot = h_full.at[other, k]
        remote(slot, slot, hf_send.at[k], hf_recv.at[other, k], {"rep": other}).wait_recv()
    head_out[...] = h_full[...]

    @pl.loop(0, nz)
    def _(b):
        for h in range(CHUNKS):
            @pl.when(jnp.logical_and(b <= z, has_right))
            def _():
                z_copy(b, 0, h).wait_send()

            @pl.when(jnp.logical_and(b >= z, has_left))
            def _():
                z_copy(b, 1, h).wait_send()

            for j in range(nx - 1):
                x_copy(b, j, h).wait_send()
            for xx in range(nx):
                c_copy(b, xx, h).wait_send()

    for j in range(nx - 1):
        wx_copy(j).wait_send()
        for i in range(ng - 1):
            wy_copy(j, i).wait_send()
        for gg in range(ng):
            wc_copy(x_peer(j), c, gg).wait_send()
    for k in range(PARTS):
        hc_copy(k).wait_send()
        hi_copy(k).wait_send()
        hf_copy(k).wait_send()

        @pl.when(jnp.logical_not(is_outer))
        def _():
            ho_copy(k).wait_send()


def finish(embed_ref, head_ref, embed_out, head_out):
    cores, parts, half, width = head_ref.shape
    embed_out[...] = embed_ref[...]
    for cc in range(cores):
        for k in range(parts):
            head_out[cc * half : (cc + 1) * half, k * width : (k + 1) * width] = head_ref[
                cc, k
            ].astype(jnp.float32)


def body(embeddings, head_weight, gp_weights, counts):
    nz, nx, nc, ng = (lax.axis_size(name) for name in ("loop", "enc", "rep", "groups"))
    rows, cols = embeddings.shape
    feats = head_weight.shape[1]
    half, width = cols // nc, feats // PARTS
    if half % (16 * ng):
        raise ValueError("head rows")
    gp_rows = gp_weights.reshape(-1, 128)
    vmem = pl.BlockSpec(memory_space=pltpu.VMEM)
    hbm = pl.BlockSpec(memory_space=pltpu.HBM)
    dma = pltpu.SemaphoreType.DMA
    embed_grad, head_sum = pl.pallas_call(
        functools.partial(kernel, (nz, nx, nc, ng)),
        out_shape=(
            jax.ShapeDtypeStruct((rows, cols), jnp.bfloat16),
            jax.ShapeDtypeStruct((nc, PARTS, half, width), jnp.bfloat16),
        ),
        in_specs=[hbm, hbm, hbm, hbm],
        out_specs=(vmem, vmem),
        scratch_shapes=[
            pltpu.VMEM(gp_rows.shape, jnp.float32),
            pltpu.SMEM(counts.shape, jnp.int32),
            pltpu.VMEM((nz, nc, nx, rows, cols), jnp.bfloat16),
            pltpu.VMEM((nx, nc, ng, half // ng, feats), jnp.bfloat16),
            pltpu.VMEM((rows, feats), jnp.bfloat16),
            pltpu.VMEM((rows, 1), jnp.float32),
            pltpu.VMEM((rows, feats), jnp.float32),
            pltpu.VMEM((rows, 1), jnp.float32),
            pltpu.VMEM((PARTS, half, width), jnp.float32),
            pltpu.VMEM((PARTS, half, width), jnp.bfloat16),
            pltpu.VMEM((PARTS, half, width), jnp.bfloat16),
            pltpu.VMEM((PARTS, half, width), jnp.bfloat16),
            pltpu.VMEM((2, PARTS, half, width), jnp.bfloat16),
            pltpu.VMEM((nc, PARTS, half, width), jnp.bfloat16),
            dma((nz, nc, nx, CHUNKS)),
            dma((2, nz, CHUNKS)),
            dma((nx - 1, nz, CHUNKS)),
            dma((nz, nx, CHUNKS)),
            dma((nx - 1,)),
            dma((nx, ng)),
            dma((nx - 1, max(ng - 1, 1))),
            dma((nx, ng)),
            dma((nx, ng)),
            dma((3 + nc * ng,)),
            dma((PARTS,)),
            dma((PARTS,)),
            dma((PARTS,)),
            dma((2, PARTS)),
            dma((PARTS,)),
            dma((PARTS,)),
            dma((nc, PARTS)),
        ],
        compiler_params=pltpu.CompilerParams(
            collective_id=0, has_side_effects=True, vmem_limit_bytes=VMEM_BYTES
        ),
    )(embeddings, head_weight, gp_rows, counts)
    return pl.pallas_call(
        finish,
        out_shape=(
            jax.ShapeDtypeStruct((rows, cols), jnp.bfloat16),
            jax.ShapeDtypeStruct((cols, feats), jnp.float32),
        ),
        in_specs=[vmem, vmem],
        out_specs=(vmem, vmem),
        compiler_params=pltpu.CompilerParams(vmem_limit_bytes=VMEM_BYTES),
    )(embed_grad, head_sum)


def solution(mesh):
    placed = (P(("groups", "loop", "rep"), "enc"), P("enc", None), P("groups"), P("groups"))
    return jax.shard_map(
        body,
        mesh=mesh,
        in_specs=placed,
        out_specs=(P(("groups", "loop", "rep"), "enc"), P(("groups", "enc"), None)),
        check_vma=False,
    )
```
